32 devices in a mesh: tensor: 16 (over z, x, core), rows: 2 (over y).
Axes of the slice: x: 2, y: 2, z: 4, core: 2. Of those that a mesh axis runs over, the one named last changes fastest.
Arguments:
- image: bfloat16 [16, 64, 3072], P('rows', None, 'tensor'), may hold values from -6 to 6
- dw_kernel: bfloat16 [7, 7, 3072], P(None, None, 'tensor'), may hold values from -0.875 to 0.875
- dw_bias: float32 [3072], P('tensor'), may hold values from -3 to 3
- norm_gain: float32 [3072], replicated, may hold values from 0.1 to 1.9
- norm_bias: float32 [3072], replicated, may hold values from -2 to 2
- w_expand: bfloat16 [3072, 12288], P('rows', 'tensor'), may hold values from -0.15625 to 0.15625
- b_expand: float32 [12288], P('tensor'), may hold values from -3 to 3
- w_project: bfloat16 [12288, 3072], P('tensor', 'rows'), may hold values from -0.078125 to 0.078125
- b_project: float32 [3072], P('tensor'), may hold values from -3 to 3
- layer_scale: float32 [3072], P('tensor'), may hold values from 0.25 to 2
- out_grad: bfloat16 [16, 64, 3072], P('rows', None, 'tensor'), may hold values from -6 to 6
Outputs:
- result: bfloat16 [16, 64, 3072], P('rows', None, 'tensor')
- image_grad: bfloat16 [16, 64, 3072], P('rows', None, 'tensor')
- expand_grad: float32 [3072, 12288], P('rows', 'tensor')
- project_grad: float32 [12288, 3072], P('tensor', 'rows')
- kernel_grad: float32 [7, 7, 3072], P(None, None, 'tensor')
- scale_grad: float32 [3072], P('tensor')
The draws below stay inside these ranges and needn't reach their ends.
All inputs are finite; a program needn't handle non-finite values.
Results may differ from the reference program's by a relative error of at most 0.022.
Values may be sent and summed in bfloat16 or wider, within the bound.
A program may use at most 128 MiB of HBM per device.

```python
import math
import jax
import jax.numpy as jnp
from jax import lax

D = 3072
FF = 12288
KS = 7
IMG_W = 64
HEIGHT = 16
N_TENSOR = 16


def spiked(entries, rng, source, target, blocks, factor):
    owner, partner = [(jnp.arange(entries.shape[axis_at]) // (entries.shape[axis_at] // blocks)).reshape([-1 if axis == axis_at else 1 for axis in range(entries.ndim)]) for axis_at in (source, target)]
    chosen = jax.random.permutation(rng, blocks)[partner]
    strong = (owner == chosen) | (owner == (partner + blocks // 2) % blocks)
    return jnp.where(strong, factor * entries, entries)


def block_levels(rng, shape, shards, low, top_value):
    level = 1.0
    for dim, shards_of in shards:
        heights = jax.random.uniform(jax.random.fold_in(jax.random.fold_in(rng, 6), dim), (shards_of,), jnp.float32, low / len(shards), top_value / len(shards))
        level = level * jnp.repeat(jnp.exp(heights), shape[dim] // shards_of).reshape((-1,) + (1,) * (len(shape) - 1 - dim))
    return level


def noise(rng, dims, width, limit, cuts=(), dtype=jnp.bfloat16):
    drawn = width * jax.random.normal(rng, dims, jnp.float32)
    if cuts:
        drawn = drawn * block_levels(rng, dims, cuts, -0.22, 0.18)
    return jnp.clip(drawn, -limit, limit).astype(dtype)


def gaussian_with(key, extent, spread, bound, shards, heavy, kind=jnp.bfloat16):
    entries = spread * jax.random.normal(key, extent, jnp.float32)
    if shards:
        entries = entries * block_levels(key, extent, shards, -0.22, 0.18)
    return jnp.clip(spiked(entries, jax.random.fold_in(key, 3), *heavy), -bound, bound).astype(kind)


def setup_inputs(seed: int = 0) -> dict:
    arg_keys = jax.random.split(jax.random.key(seed), 12)
    image = noise(arg_keys[0], (HEIGHT, IMG_W, D), 1.0, 6.0, ((0, 2), (2, 16)))
    dw_kernel = noise(arg_keys[1], (KS, KS, D), (KS * KS) ** -0.5, 0.875, ((2, 16),))
    dw_bias = noise(arg_keys[2], (D,), 0.5, 3.0, ((0, 16),), jnp.float32)
    norm_gain = jnp.clip(1.0 + 0.18 * jax.random.normal(arg_keys[3], (D,), jnp.float32), 0.1, 1.9)
    norm_bias = noise(arg_keys[4], (D,), 0.3, 2.0, (), jnp.float32)
    w_expand = gaussian_with(arg_keys[5], (D, FF), D ** -0.5, 0.15625, ((0, 2), (1, 16)), (1, 0, 16, 2.0))
    b_expand = noise(arg_keys[6], (FF,), 0.5, 3.0, ((0, 16),), jnp.float32)
    w_project = gaussian_with(arg_keys[7], (FF, D), FF ** -0.5, 0.078125, ((0, 16), (1, 2)), (0, 1, 16, 2.0))
    b_project = noise(arg_keys[8], (D,), 0.5, 3.0, ((0, 16),), jnp.float32)
    layer_scale = jnp.clip(jnp.exp(math.log(2.0) - 2.0794415 * jax.random.uniform(arg_keys[9], (D,), jnp.float32) ** block_levels(arg_keys[9], (D,), ((0, 16),), -0.2, 0.2)), 0.25, 2.0)
    out_grad = noise(arg_keys[10], (HEIGHT, IMG_W, D), 1.0, 6.0, ((0, 2), (2, 16)))
    return dict(image=image, dw_kernel=dw_kernel, dw_bias=dw_bias, norm_gain=norm_gain, norm_bias=norm_bias, w_expand=w_expand, b_expand=b_expand, w_project=w_project, b_project=b_project, layer_scale=layer_scale, out_grad=out_grad)


EPSILON = 1e-06

def gelu_exact(values):
    return 0.5 * values * (1.0 + lax.erf(values * (1.0 / math.sqrt(2.0))))

def gelu_slope(values):
    cumulative = 0.5 * (1.0 + lax.erf(values * (1.0 / math.sqrt(2.0))))
    density = jnp.exp(-0.5 * values * values) * (1.0 / math.sqrt(2.0 * math.pi))
    return cumulative + values * density

def depthwise(padded, kernel, height, breadth):
    kernel_size = kernel.shape[0]
    summed = jnp.zeros((height, breadth, kernel.shape[2]), jnp.float32)
    for row_shift in range(kernel_size):
        for col_shift in range(kernel_size):
            window = padded[row_shift:row_shift + height, col_shift:col_shift + breadth]
            summed = summed + kernel[row_shift, col_shift].astype(jnp.float32) * window
    return summed

def kernel_terms(padded, gradient, kernel_size):
    height, breadth = (gradient.shape[0], gradient.shape[1])
    kernel_rows = []
    for row_shift in range(kernel_size):
        kernel_line = []
        for col_shift in range(kernel_size):
            window = padded[row_shift:row_shift + height, col_shift:col_shift + breadth]
            kernel_line.append(lax.optimization_barrier(jnp.sum(window * gradient, axis=(0, 1))))
        kernel_rows.append(jnp.stack(kernel_line))
    return jnp.stack(kernel_rows)

def grouped_product(left, right):
    groups = N_TENSOR
    span = left.shape[1] // groups
    left_blocks = jnp.transpose(left.reshape(left.shape[0], groups, span), (1, 0, 2))
    right_blocks = right.reshape(groups, span, right.shape[1])

    def add_group(summed, blocks):
        term = jnp.dot(blocks[0], blocks[1], preferred_element_type=jnp.float32)
        rounded = lax.optimization_barrier(term.astype(jnp.bfloat16))
        return (summed + rounded.astype(jnp.float32), None)
    start = jnp.zeros((left.shape[0], right.shape[1]), jnp.float32)
    summed, unused = lax.scan(add_group, start, (left_blocks, right_blocks))
    return summed

def reference(image, dw_kernel, dw_bias, norm_gain, norm_bias, w_expand, b_expand, w_project, b_project, layer_scale, out_grad):
    height, breadth, features = image.shape
    positions = height * breadth
    rim_depth = dw_kernel.shape[0] // 2
    padded_image = jnp.pad(image.astype(jnp.float32), ((rim_depth, rim_depth), (rim_depth, rim_depth), (0, 0)))
    convolved = depthwise(padded_image, dw_kernel, height, breadth) + dw_bias
    mixed = convolved.astype(jnp.bfloat16).reshape(positions, features).astype(jnp.float32)
    average = lax.optimization_barrier(jnp.sum(mixed, 1, keepdims=True)) / features
    mean_square = lax.optimization_barrier(jnp.sum(mixed * mixed, 1, keepdims=True)) / features
    inv_std = lax.rsqrt(mean_square - average * average + EPSILON)
    centred = (mixed - average) * inv_std
    normed = (centred * norm_gain + norm_bias).astype(jnp.bfloat16)
    pre = jnp.dot(normed, w_expand, preferred_element_type=jnp.float32) + b_expand
    hidden = gelu_exact(pre).astype(jnp.bfloat16)
    projected = grouped_product(hidden, w_project) + b_project
    residual = image.reshape(positions, features).astype(jnp.float32)
    result = (residual + layer_scale * projected).astype(jnp.bfloat16).reshape(height, breadth, features)
    upstream = out_grad.reshape(positions, features).astype(jnp.float32)
    scale_grad = lax.optimization_barrier(jnp.sum(upstream * projected, 0))
    scaled_grad = (upstream * layer_scale).astype(jnp.bfloat16)
    project_grad = jnp.dot(hidden.T, scaled_grad, preferred_element_type=jnp.float32)
    hidden_grad = jnp.dot(scaled_grad, w_project.T, preferred_element_type=jnp.float32)
    pre_grad = (hidden_grad * gelu_slope(pre)).astype(jnp.bfloat16)
    expand_grad = jnp.dot(normed.T, pre_grad, preferred_element_type=jnp.float32)
    normed_grad = grouped_product(pre_grad, w_expand.T)
    gain_grad = normed_grad * norm_gain
    plain_mean = lax.optimization_barrier(jnp.sum(gain_grad, 1, keepdims=True)) / features
    centred_mean = lax.optimization_barrier(jnp.sum(gain_grad * centred, 1, keepdims=True)) / features
    mixed_grad = (inv_std * (gain_grad - plain_mean - centred * centred_mean)).astype(jnp.bfloat16)
    mixed_grad = mixed_grad.reshape(height, breadth, features).astype(jnp.float32)
    padded_grad = jnp.pad(mixed_grad, ((rim_depth, rim_depth), (rim_depth, rim_depth), (0, 0)))
    back = depthwise(padded_grad, dw_kernel[::-1, ::-1], height, breadth)
    image_grad = (upstream.reshape(height, breadth, features) + back).astype(jnp.bfloat16)
    kernel_grad = kernel_terms(padded_image, mixed_grad, dw_kernel.shape[0])
    return (result, image_grad, expand_grad, project_grad, kernel_grad, scale_grad)
```

```python
import math

import jax
import jax.numpy as jnp
from jax import lax
from jax.sharding import PartitionSpec as P

EPSILON = 1e-06


def extended(cells, sides, width):
    for axis, dim in sides:
        count = lax.axis_size(axis)
        ends = count - 1
        head = lax.slice_in_dim(cells, 0, width, axis=dim)
        tail = lax.slice_in_dim(cells, cells.shape[dim] - width, cells.shape[dim], axis=dim)
        cells = jnp.concatenate(
            [
                lax.ppermute(tail, axis, [(i, (i + 1) % count) for i in range(ends)]),
                cells,
                lax.ppermute(head, axis, [((i + 1) % count, i) for i in range(ends)]),
            ],
            axis=dim,
        )
    return cells


def gelu_exact(values):
    return 0.5 * values * (1.0 + lax.erf(values * (1.0 / math.sqrt(2.0))))


def gelu_slope(values):
    cumulative = 0.5 * (1.0 + lax.erf(values * (1.0 / math.sqrt(2.0))))
    density = jnp.exp(-0.5 * values * values) * (1.0 / math.sqrt(2.0 * math.pi))
    return cumulative + values * density


def depthwise(padded, kernel, height, breadth):
    kernel_size = kernel.shape[0]
    summed = jnp.zeros((height, breadth, kernel.shape[2]), jnp.float32)
    for row_shift in range(kernel_size):
        for col_shift in range(kernel_size):
            window = padded[row_shift : row_shift + height, col_shift : col_shift + breadth]
            summed = summed + kernel[row_shift, col_shift].astype(jnp.float32) * window
    return summed


def kernel_terms(padded, gradient, kernel_size):
    height, breadth = (gradient.shape[0], gradient.shape[1])
    kernel_rows = []
    for row_shift in range(kernel_size):
        kernel_line = []
        for col_shift in range(kernel_size):
            window = padded[row_shift : row_shift + height, col_shift : col_shift + breadth]
            kernel_line.append(jnp.sum(window * gradient, axis=(0, 1)))
        kernel_rows.append(jnp.stack(kernel_line))
    return jnp.stack(kernel_rows)


def contract_last(left, right):
    return lax.dot_general(
        left, right, (((1,), (1,)), ((), ())), preferred_element_type=jnp.float32
    )


def contract_first(left, right):
    return lax.dot_general(
        left, right, (((0,), (0,)), ((), ())), preferred_element_type=jnp.float32
    )


def general_plan(
    image,
    dw_kernel,
    dw_bias,
    norm_gain,
    norm_bias,
    w_expand,
    b_expand,
    w_project,
    b_project,
    layer_scale,
    out_grad,
):
    kernel_size = dw_kernel.shape[0]
    rim_depth = kernel_size // 2
    height, breadth, channels = image.shape
    positions = height * breadth
    features = norm_gain.shape[0]
    channel_start = lax.axis_index("tensor") * channels
    gain_part = lax.dynamic_slice_in_dim(norm_gain, channel_start, channels)
    shift_part = lax.dynamic_slice_in_dim(norm_bias, channel_start, channels)
    rimmed = extended(image, (("rows", 0),), rim_depth)
    wide_image = jnp.pad(rimmed, ((0, 0), (rim_depth, rim_depth), (0, 0))).astype(jnp.float32)
    convolved = depthwise(wide_image, dw_kernel, height, breadth) + dw_bias
    mixed = convolved.astype(jnp.bfloat16).reshape(positions, channels)
    own_mixed = mixed.astype(jnp.float32)
    plain_sum, square_sum = lax.psum(
        (jnp.sum(own_mixed, 1), jnp.sum(own_mixed * own_mixed, 1)), "tensor"
    )
    average = plain_sum[:, None] / features
    inv_std = lax.rsqrt(square_sum[:, None] / features - average * average + EPSILON)
    centred = (own_mixed - average) * inv_std
    normed_part = (centred * gain_part + shift_part).astype(jnp.bfloat16)
    normed = lax.all_gather(normed_part, "tensor", axis=1, tiled=True)
    columns = normed
    pre = jnp.dot(
        columns,
        lax.all_gather(w_expand, "rows", axis=0, tiled=True),
        preferred_element_type=jnp.float32,
    )
    pre = pre + b_expand
    hidden = gelu_exact(pre).astype(jnp.bfloat16)
    partial_out = jnp.dot(
        hidden,
        lax.all_gather(w_project, "rows", axis=1, tiled=True),
        preferred_element_type=jnp.float32,
    )
    projected = (
        lax.psum_scatter(
            partial_out.astype(jnp.bfloat16), "tensor", scatter_dimension=1, tiled=True
        ).astype(jnp.float32)
        + b_project
    )
    residual = image.reshape(positions, channels).astype(jnp.float32)
    result = (
        (residual + layer_scale * projected).astype(jnp.bfloat16).reshape(height, breadth, channels)
    )
    upstream = out_grad.reshape(positions, channels).astype(jnp.float32)
    scale_term = jnp.sum(upstream * projected, 0)
    scaled_grad = (upstream * layer_scale).astype(jnp.bfloat16)
    grad_panels = lax.all_gather(scaled_grad, "tensor", axis=1, tiled=True)
    project_term = contract_first(hidden, grad_panels)
    project_grad = lax.psum_scatter(
        project_term.astype(jnp.bfloat16), "rows", scatter_dimension=1, tiled=True
    ).astype(jnp.float32)
    columns = grad_panels
    hidden_grad = contract_last(columns, lax.all_gather(w_project, "rows", axis=1, tiled=True))
    pre_grad = (hidden_grad * gelu_slope(pre)).astype(jnp.bfloat16)
    columns = normed
    expand_grad = lax.psum_scatter(
        contract_first(columns, pre_grad).astype(jnp.bfloat16),
        "rows",
        scatter_dimension=0,
        tiled=True,
    ).astype(jnp.float32)
    normed_partial = contract_last(pre_grad, lax.all_gather(w_expand, "rows", axis=0, tiled=True))
    normed_grad = lax.psum_scatter(
        normed_partial.astype(jnp.bfloat16), "tensor", scatter_dimension=1, tiled=True
    ).astype(jnp.float32)
    gain_grad = normed_grad * gain_part
    plain_total, centred_total = lax.psum(
        (jnp.sum(gain_grad, 1), jnp.sum(gain_grad * centred, 1)), "tensor"
    )
    plain_mean = plain_total[:, None] / features
    centred_mean = centred_total[:, None] / features
    mixed_grad = (inv_std * (gain_grad - plain_mean - centred * centred_mean)).astype(jnp.bfloat16)
    mixed_grad = mixed_grad.reshape(height, breadth, channels)
    grad_rimmed = extended(mixed_grad, (("rows", 0),), rim_depth)
    wide_grad = jnp.pad(grad_rimmed, ((0, 0), (rim_depth, rim_depth), (0, 0))).astype(jnp.float32)
    back = depthwise(wide_grad, dw_kernel[::-1, ::-1], height, breadth)
    image_grad = (upstream.reshape(height, breadth, channels) + back).astype(jnp.bfloat16)
    kernel_local = kernel_terms(wide_image, mixed_grad.astype(jnp.float32), kernel_size)
    kernel_grad, scale_grad = lax.psum((kernel_local, scale_term), "rows")
    return (result, image_grad, expand_grad, project_grad, kernel_grad, scale_grad)


def pair_swap(value):
    return lax.ppermute(value, "rows", [(0, 1), (1, 0)])


def trade_blocks(block):
    count = lax.axis_size("tensor")
    half = count // 2
    pairs = []
    for low in range(half):
        first, second = 2 * low + 1, 2 * (low + half)
        pairs += [(first, second), (second, first)]
    other = lax.ppermute(block, ("tensor", "rows"), pairs)
    upper = lax.axis_index("tensor") >= half
    stays = upper == (lax.axis_index("rows") == 1)
    return jnp.where(stays, block, other)


def gather_plane(block):
    count = lax.axis_size("tensor")
    positions, channels = block.shape
    gathered = lax.all_gather(trade_blocks(block), "tensor", axis=0)
    gathered = gathered.reshape(2, count // 2, positions, channels)
    return gathered.transpose(0, 2, 1, 3).reshape(2 * positions, count // 2 * channels)


def scatter_plane(partial):
    count = lax.axis_size("tensor")
    positions, channels = partial.shape[0] // 2, partial.shape[1] // (count // 2)
    blocks = partial.reshape(2, positions, count // 2, channels).transpose(0, 2, 1, 3)
    blocks = blocks.reshape(count, positions, channels)
    return trade_blocks(lax.psum_scatter(blocks, "tensor", scatter_dimension=0, tiled=False))


def paired_plan(
    image,
    dw_kernel,
    dw_bias,
    norm_gain,
    norm_bias,
    w_expand,
    b_expand,
    w_project,
    b_project,
    layer_scale,
    out_grad,
):
    kernel_size = dw_kernel.shape[0]
    rim_depth = kernel_size // 2
    height, breadth, channels = image.shape
    positions = height * breadth
    features = norm_gain.shape[0]
    half_features = features // 2
    row = lax.axis_index("rows")
    channel_start = lax.axis_index("tensor") * channels
    gain_part = lax.dynamic_slice_in_dim(norm_gain, channel_start, channels)
    gain_half = lax.dynamic_slice_in_dim(norm_gain, row * half_features, half_features)
    shift_half = lax.dynamic_slice_in_dim(norm_bias, row * half_features, half_features)
    upstream = out_grad.reshape(positions, channels).astype(jnp.float32)
    scaled_grad = (upstream * layer_scale).astype(jnp.bfloat16)
    grad_panels = gather_plane(scaled_grad)
    rimmed = extended(image, (("rows", 0),), rim_depth)
    wide_image = jnp.pad(rimmed, ((0, 0), (rim_depth, rim_depth), (0, 0))).astype(jnp.float32)
    convolved = depthwise(wide_image, dw_kernel, height, breadth) + dw_bias
    mixed = convolved.astype(jnp.bfloat16).reshape(positions, channels)
    mixed_panels = gather_plane(mixed)
    hidden_partial = contract_last(grad_panels, w_project)
    hidden_grad = hidden_partial + pair_swap(hidden_partial.astype(jnp.bfloat16))
    mixed_wide = mixed_panels.astype(jnp.float32)
    sums = jnp.stack([jnp.sum(mixed_wide, 1), jnp.sum(mixed_wide * mixed_wide, 1)])
    sums = sums + pair_swap(sums)
    average = sums[0] / features
    inv_std = lax.rsqrt(sums[1] / features - average * average + EPSILON)
    centred_half = (mixed_wide - average[:, None]) * inv_std[:, None]
    normed = (centred_half * gain_half + shift_half).astype(jnp.bfloat16)
    pre_partial = jnp.dot(normed, w_expand, preferred_element_type=jnp.float32)
    pre = pre_partial + pair_swap(pre_partial.astype(jnp.bfloat16)) + b_expand
    pre_grad = (hidden_grad * gelu_slope(pre)).astype(jnp.bfloat16)
    normed_partial = contract_last(pre_grad, w_expand)
    normed_grad = scatter_plane(normed_partial.astype(jnp.bfloat16)).astype(jnp.float32)
    hidden = gelu_exact(pre).astype(jnp.bfloat16)
    partial_out = jnp.dot(hidden, w_project, preferred_element_type=jnp.float32)
    projected = scatter_plane(partial_out.astype(jnp.bfloat16)).astype(jnp.float32) + b_project
    project_grad = contract_first(hidden, grad_panels)
    expand_grad = contract_first(normed, pre_grad)
    residual = image.reshape(positions, channels).astype(jnp.float32)
    result = (
        (residual + layer_scale * projected).astype(jnp.bfloat16).reshape(height, breadth, channels)
    )
    scale_term = jnp.sum(upstream * projected, 0)
    own_average = lax.dynamic_slice_in_dim(average, row * positions, positions)[:, None]
    own_inv_std = lax.dynamic_slice_in_dim(inv_std, row * positions, positions)[:, None]
    centred = (mixed.astype(jnp.float32) - own_average) * own_inv_std
    gain_grad = normed_grad * gain_part
    plain_total, centred_total = lax.psum(
        (jnp.sum(gain_grad, 1), jnp.sum(gain_grad * centred, 1)), "tensor"
    )
    plain_mean = plain_total[:, None] / features
    centred_mean = centred_total[:, None] / features
    mixed_grad = (own_inv_std * (gain_grad - plain_mean - centred * centred_mean)).astype(
        jnp.bfloat16
    )
    mixed_grad = mixed_grad.reshape(height, breadth, channels)
    grad_rimmed = extended(mixed_grad, (("rows", 0),), rim_depth)
    wide_grad = jnp.pad(grad_rimmed, ((0, 0), (rim_depth, rim_depth), (0, 0))).astype(jnp.float32)
    back = depthwise(wide_grad, dw_kernel[::-1, ::-1], height, breadth)
    image_grad = (upstream.reshape(height, breadth, channels) + back).astype(jnp.bfloat16)
    kernel_local = kernel_terms(wide_image, mixed_grad.astype(jnp.float32), kernel_size)
    kernel_grad = kernel_local + pair_swap(kernel_local)
    scale_grad = scale_term + pair_swap(scale_term)
    return (result, image_grad, expand_grad, project_grad, kernel_grad, scale_grad)


def solution(mesh):
    paired = mesh.shape["rows"] == 2 and mesh.shape["tensor"] % 2 == 0
    return jax.shard_map(
        paired_plan if paired else general_plan,
        mesh=mesh,
        in_specs=(
            P("rows", None, "tensor"),
            P(None, None, "tensor"),
            P("tensor"),
            P(),
            P(),
            P("rows", "tensor"),
            P("tensor"),
            P("tensor", "rows"),
            P("tensor"),
            P("tensor"),
            P("rows", None, "tensor"),
        ),
        out_specs=(
            P("rows", None, "tensor"),
            P("rows", None, "tensor"),
            P("rows", "tensor"),
            P("tensor", "rows"),
            P(None, None, "tensor"),
            P("tensor"),
        ),
        check_vma=False,
    )
```

```python
import functools
import math

import jax
import jax.numpy as jnp
from jax import lax
from jax.experimental import pallas as pl
from jax.experimental.pallas import tpu as pltpu
from jax.sharding import PartitionSpec as P

EPSILON = 1e-06


def extended(cells, sides, width):
    for axis, dim in sides:
        count = lax.axis_size(axis)
        ends = count - 1
        head = lax.slice_in_dim(cells, 0, width, axis=dim)
        tail = lax.slice_in_dim(cells, cells.shape[dim] - width, cells.shape[dim], axis=dim)
        cells = jnp.concatenate(
            [
                lax.ppermute(tail, axis, [(i, (i + 1) % count) for i in range(ends)]),
                cells,
                lax.ppermute(head, axis, [((i + 1) % count, i) for i in range(ends)]),
            ],
            axis=dim,
        )
    return cells


def gelu_exact(values):
    return 0.5 * values * (1.0 + lax.erf(values * (1.0 / math.sqrt(2.0))))


def gelu_slope(values):
    cumulative = 0.5 * (1.0 + lax.erf(values * (1.0 / math.sqrt(2.0))))
    density = jnp.exp(-0.5 * values * values) * (1.0 / math.sqrt(2.0 * math.pi))
    return cumulative + values * density


def depthwise(padded, kernel, height, breadth):
    kernel_size = kernel.shape[0]
    summed = jnp.zeros((height, breadth, kernel.shape[2]), jnp.float32)
    for row_shift in range(kernel_size):
        for col_shift in range(kernel_size):
            window = padded[row_shift : row_shift + height, col_shift : col_shift + breadth]
            summed = summed + kernel[row_shift, col_shift].astype(jnp.float32) * window
    return summed


def kernel_terms(padded, gradient, kernel_size):
    height, breadth = (gradient.shape[0], gradient.shape[1])
    kernel_rows = []
    for row_shift in range(kernel_size):
        kernel_line = []
        for col_shift in range(kernel_size):
            window = padded[row_shift : row_shift + height, col_shift : col_shift + breadth]
            kernel_line.append(jnp.sum(window * gradient, axis=(0, 1)))
        kernel_rows.append(jnp.stack(kernel_line))
    return jnp.stack(kernel_rows)


def contract_last(left, right):
    return lax.dot_general(
        left, right, (((1,), (1,)), ((), ())), preferred_element_type=jnp.float32
    )


def contract_first(left, right):
    return lax.dot_general(
        left, right, (((0,), (0,)), ((), ())), preferred_element_type=jnp.float32
    )


def general_plan(
    image,
    dw_kernel,
    dw_bias,
    norm_gain,
    norm_bias,
    w_expand,
    b_expand,
    w_project,
    b_project,
    layer_scale,
    out_grad,
):
    kernel_size = dw_kernel.shape[0]
    rim_depth = kernel_size // 2
    height, breadth, channels = image.shape
    positions = height * breadth
    features = norm_gain.shape[0]
    channel_start = lax.axis_index("tensor") * channels
    gain_part = lax.dynamic_slice_in_dim(norm_gain, channel_start, channels)
    shift_part = lax.dynamic_slice_in_dim(norm_bias, channel_start, channels)
    rimmed = extended(image, (("rows", 0),), rim_depth)
    wide_image = jnp.pad(rimmed, ((0, 0), (rim_depth, rim_depth), (0, 0))).astype(jnp.float32)
    convolved = depthwise(wide_image, dw_kernel, height, breadth) + dw_bias
    mixed = convolved.astype(jnp.bfloat16).reshape(positions, channels)
    own_mixed = mixed.astype(jnp.float32)
    plain_sum, square_sum = lax.psum(
        (jnp.sum(own_mixed, 1), jnp.sum(own_mixed * own_mixed, 1)), "tensor"
    )
    average = plain_sum[:, None] / features
    inv_std = lax.rsqrt(square_sum[:, None] / features - average * average + EPSILON)
    centred = (own_mixed - average) * inv_std
    normed_part = (centred * gain_part + shift_part).astype(jnp.bfloat16)
    normed = lax.all_gather(normed_part, "tensor", axis=1, tiled=True)
    columns = normed
    pre = jnp.dot(
        columns,
        lax.all_gather(w_expand, "rows", axis=0, tiled=True),
        preferred_element_type=jnp.float32,
    )
    pre = pre + b_expand
    hidden = gelu_exact(pre).astype(jnp.bfloat16)
    partial_out = jnp.dot(
        hidden,
        lax.all_gather(w_project, "rows", axis=1, tiled=True),
        preferred_element_type=jnp.float32,
    )
    projected = (
        lax.psum_scatter(
            partial_out.astype(jnp.bfloat16), "tensor", scatter_dimension=1, tiled=True
        ).astype(jnp.float32)
        + b_project
    )
    residual = image.reshape(positions, channels).astype(jnp.float32)
    result = (
        (residual + layer_scale * projected).astype(jnp.bfloat16).reshape(height, breadth, channels)
    )
    upstream = out_grad.reshape(positions, channels).astype(jnp.float32)
    scale_term = jnp.sum(upstream * projected, 0)
    scaled_grad = (upstream * layer_scale).astype(jnp.bfloat16)
    grad_panels = lax.all_gather(scaled_grad, "tensor", axis=1, tiled=True)
    project_term = contract_first(hidden, grad_panels)
    project_grad = lax.psum_scatter(
        project_term.astype(jnp.bfloat16), "rows", scatter_dimension=1, tiled=True
    ).astype(jnp.float32)
    columns = grad_panels
    hidden_grad = contract_last(columns, lax.all_gather(w_project, "rows", axis=1, tiled=True))
    pre_grad = (hidden_grad * gelu_slope(pre)).astype(jnp.bfloat16)
    columns = normed
    expand_grad = lax.psum_scatter(
        contract_first(columns, pre_grad).astype(jnp.bfloat16),
        "rows",
        scatter_dimension=0,
        tiled=True,
    ).astype(jnp.float32)
    normed_partial = contract_last(pre_grad, lax.all_gather(w_expand, "rows", axis=0, tiled=True))
    normed_grad = lax.psum_scatter(
        normed_partial.astype(jnp.bfloat16), "tensor", scatter_dimension=1, tiled=True
    ).astype(jnp.float32)
    gain_grad = normed_grad * gain_part
    plain_total, centred_total = lax.psum(
        (jnp.sum(gain_grad, 1), jnp.sum(gain_grad * centred, 1)), "tensor"
    )
    plain_mean = plain_total[:, None] / features
    centred_mean = centred_total[:, None] / features
    mixed_grad = (inv_std * (gain_grad - plain_mean - centred * centred_mean)).astype(jnp.bfloat16)
    mixed_grad = mixed_grad.reshape(height, breadth, channels)
    grad_rimmed = extended(mixed_grad, (("rows", 0),), rim_depth)
    wide_grad = jnp.pad(grad_rimmed, ((0, 0), (rim_depth, rim_depth), (0, 0))).astype(jnp.float32)
    back = depthwise(wide_grad, dw_kernel[::-1, ::-1], height, breadth)
    image_grad = (upstream.reshape(height, breadth, channels) + back).astype(jnp.bfloat16)
    kernel_local = kernel_terms(wide_image, mixed_grad.astype(jnp.float32), kernel_size)
    kernel_grad, scale_grad = lax.psum((kernel_local, scale_term), "rows")
    return (result, image_grad, expand_grad, project_grad, kernel_grad, scale_grad)


def pair_swap(value):
    return lax.ppermute(value, "rows", [(0, 1), (1, 0)])


MESH = pl.DeviceIdType.MESH
CHIP_STEPS = (2, 1, 3)


class Place:
    def __init__(self):
        self.tensor = lax.axis_index("tensor")
        self.row = lax.axis_index("rows")
        self.core = lax.rem(self.tensor, 2)
        self.column = lax.rem(self.tensor // 2, 2)
        self.count = lax.axis_size("tensor")
        self.across = self.tensor + 2 - 4 * self.column
        self.sibling = self.tensor + 1 - 2 * self.core
        self.traded = (self.tensor // (self.count // 2)) != self.row
        self.trader = lax.rem(self.tensor + self.count // 2, self.count)

    def along(self, step):
        return lax.rem(self.tensor + 4 * step, self.count)

    def here(self, tensor):
        return (tensor, self.row)

    def meet(self):
        barrier = pltpu.get_barrier_semaphore()
        peers = [self.sibling, self.across] + [self.along(step) for step in CHIP_STEPS]
        for peer in peers:
            pl.semaphore_signal(barrier, inc=1, device_id=self.here(peer), device_id_type=MESH)

        pl.semaphore_signal(
            barrier, inc=1, device_id=(self.trader, 1 - self.row), device_id_type=MESH
        )
        pl.semaphore_wait(barrier, len(peers) + 1)


def remote(source, target, sems, device):
    return pltpu.make_async_remote_copy(
        src_ref=source,
        dst_ref=target,
        send_sem=sems.at[0],
        recv_sem=sems.at[1],
        device_id=device,
        device_id_type=MESH,
    )


def region(ref, tensor, core, quarter, width, count):
    half = tensor // (count // 2)
    panel = lax.rem(tensor, count // 2) // 2
    rows = pl.ds(pl.multiple_of(half * 2 * quarter + core * quarter, quarter), quarter)
    return ref.at[rows, pl.ds(pl.multiple_of(panel * width, 128), width)]


def gather_kernel(block_ref, out_ref, arrived, block, pre_sem, swap_sem, z_sem, x_sem, c_sem):
    place = Place()
    quarter = block_ref.shape[0] // 2
    width = block.shape[1]

    def spot(tensor):
        return region(out_ref, tensor, place.core, quarter, width, place.count)

    place.meet()
    other_rows = pl.ds(pl.multiple_of((1 - place.core) * quarter, quarter), quarter)
    own_rows = pl.ds(pl.multiple_of(place.core * quarter, quarter), quarter)
    pairing = remote(block_ref.at[other_rows, :], arrived, pre_sem, place.here(place.sibling))
    pairing.start()
    pairing.wait()

    @pl.when(place.core == 0)
    def _():
        block[...] = jnp.concatenate([block_ref[own_rows, :], arrived[...]], axis=1)

    @pl.when(place.core == 1)
    def _():
        block[...] = jnp.concatenate([arrived[...], block_ref[own_rows, :]], axis=1)

    @pl.when(place.traded)
    def _():
        swap = remote(block, spot(place.trader), swap_sem, (place.trader, 1 - place.row))
        swap.start()
        swap.wait()

    @pl.when(jnp.logical_not(place.traded))
    def _():
        keep = pltpu.make_async_copy(block, spot(place.tensor), swap_sem.at[0])
        keep.start()
        keep.wait()

    mine = spot(place.tensor)
    z_copies = [
        remote(mine, mine, z_sem.at[step], place.here(place.along(step))) for step in CHIP_STEPS
    ]
    for copy in z_copies:
        copy.start()
    x_copies, c_copies = [], []
    for index, step in enumerate((0,) + CHIP_STEPS):
        if step:
            z_copies[index - 1].wait_recv()
        origin = lax.rem(place.tensor + 4 * (4 - step), place.count)
        chunk = spot(origin)
        x_copies.append(remote(chunk, chunk, x_sem.at[index], place.here(place.across)))
        c_copies.append(remote(chunk, chunk, c_sem.at[index], place.here(place.sibling)))
        x_copies[-1].start()
        c_copies[-1].start()
    for index, step in enumerate((0,) + CHIP_STEPS):
        x_copies[index].wait_recv()
        origin = lax.rem(place.across + 4 * (4 - step), place.count)
        chunk = spot(origin)
        c_copies.append(remote(chunk, chunk, c_sem.at[4 + index], place.here(place.sibling)))
        c_copies[-1].start()
    for copy in c_copies:
        copy.wait_recv()
    for copy in z_copies + x_copies + c_copies:
        copy.wait_send()


def gather_plane(block, collective_id):
    count = lax.axis_size("tensor")
    positions, channels = block.shape
    quarter, width = positions // 2, 2 * channels
    dma = pltpu.SemaphoreType.DMA
    return pl.pallas_call(
        gather_kernel,
        out_shape=jax.ShapeDtypeStruct((2 * positions, count // 2 * channels), block.dtype),
        in_specs=[pl.BlockSpec(memory_space=pltpu.VMEM)],
        out_specs=pl.BlockSpec(memory_space=pltpu.VMEM),
        scratch_shapes=[
            pltpu.VMEM((quarter, channels), block.dtype),
            pltpu.VMEM((quarter, width), block.dtype),
            dma((2,)),
            dma((2,)),
            dma((4, 2)),
            dma((4, 2)),
            dma((8, 2)),
        ],
        compiler_params=pltpu.CompilerParams(
            collective_id=collective_id, has_side_effects=True, vmem_limit_bytes=24 * 2**20
        ),
        name="gather_plane",
    )(block)


def scatter_kernel(arrays, *refs):
    partials, outs = refs[:arrays], refs[arrays : 2 * arrays]
    from_core, to_x, from_x, to_z, from_z, kept, final, swapped, leaving = refs[
        2 * arrays : 2 * arrays + 9
    ]
    c_sem, x_sem, z_sem, swap_sem, end_sem = refs[2 * arrays + 9 :]
    place = Place()
    quarter, width = final.shape[1:]
    channels = width // 2
    place.meet()
    copies = []
    c_copies = []
    for a in range(arrays):
        for half in range(2):
            start = half * 2 * quarter + (1 - place.core) * quarter
            rows = pl.ds(pl.multiple_of(start, quarter), quarter)
            copy = remote(
                partials[a].at[rows, :],
                from_core.at[a, half],
                c_sem.at[a, half],
                place.here(place.sibling),
            )
            copy.start()
            c_copies.append(copy)

    def chip_sum(a, tensor):
        half = tensor // (place.count // 2)
        panel = lax.rem(tensor, place.count // 2) // 2
        lanes = pl.ds(pl.multiple_of(panel * width, 128), width)
        start = half * 2 * quarter + place.core * quarter
        rows = pl.ds(pl.multiple_of(start, quarter), quarter)
        own = partials[a][rows, lanes].astype(jnp.float32)
        return own + from_core[a, half, :, lanes].astype(jnp.float32)

    x_copies, z_copies = {}, {}
    for a in range(arrays):
        c_copies[2 * a].wait_recv()
        c_copies[2 * a + 1].wait_recv()
        for step in CHIP_STEPS + (0,):
            target = lax.rem(place.across + 4 * step, place.count)
            to_x[a, step] = chip_sum(a, target).astype(to_x.dtype)
            copy = remote(
                to_x.at[a, step], from_x.at[a, step], x_sem.at[a, step], place.here(place.across)
            )
            copy.start()
            x_copies[a, step] = copy
    for a in range(arrays):
        for step in CHIP_STEPS + (0,):
            target = place.along(step)
            x_copies[a, step].wait_recv()
            summed = chip_sum(a, target) + from_x[a, step].astype(jnp.float32)
            if step:
                to_z[a, step] = summed.astype(to_z.dtype)
                copy = remote(
                    to_z.at[a, step], from_z.at[a, step], z_sem.at[a, step], place.here(target)
                )
                copy.start()
                z_copies[a, step] = copy
            else:
                kept[a] = summed
    swaps = []
    for a in range(arrays):
        summed = kept[a]
        for step in CHIP_STEPS:
            z_copies[a, step].wait_recv()
            summed = summed + from_z[a, step].astype(jnp.float32)
        final[a] = summed.astype(final.dtype)
        swap = remote(
            final.at[a], swapped.at[a], swap_sem.at[a], (place.trader, 1 - place.row)
        )
        swaps.append(swap)

        @pl.when(place.traded)
        def _():
            swap.start()

    ends = []
    own_rows = pl.ds(pl.multiple_of(place.core * quarter, quarter), quarter)
    for a in range(arrays):

        @pl.when(place.traded)
        def _():
            swaps[a].wait()

        @pl.when(jnp.logical_not(place.traded))
        def _():
            swapped[a] = final[a]

        @pl.when(place.core == 0)
        def _():
            outs[a][own_rows, :] = swapped[a][:, :channels]
            leaving[a] = swapped[a][:, channels:]

        @pl.when(place.core == 1)
        def _():
            outs[a][own_rows, :] = swapped[a][:, channels:]
            leaving[a] = swapped[a][:, :channels]

        copy = remote(
            leaving.at[a], outs[a].at[own_rows, :], end_sem.at[a], place.here(place.sibling)
        )
        copy.start()
        ends.append(copy)
    for copy in ends:
        copy.wait()
    for copy in c_copies + list(x_copies.values()) + list(z_copies.values()):
        copy.wait_send()


def scatter_plane(partials, collective_id):
    count = lax.axis_size("tensor")
    arrays = len(partials)
    positions, channels = partials[0].shape[0] // 2, partials[0].shape[1] // (count // 2)
    quarter, width = positions // 2, 2 * channels
    dma = pltpu.SemaphoreType.DMA
    kind = partials[0].dtype
    vmem = pl.BlockSpec(memory_space=pltpu.VMEM)
    return pl.pallas_call(
        functools.partial(scatter_kernel, arrays),
        out_shape=[jax.ShapeDtypeStruct((positions, channels), kind)] * arrays,
        in_specs=[vmem] * arrays,
        out_specs=[vmem] * arrays,
        scratch_shapes=[
            pltpu.VMEM((arrays, 2, quarter, partials[0].shape[1]), kind),
            pltpu.VMEM((arrays, 4, quarter, width), kind),
            pltpu.VMEM((arrays, 4, quarter, width), kind),
            pltpu.VMEM((arrays, 4, quarter, width), kind),
            pltpu.VMEM((arrays, 4, quarter, width), kind),
            pltpu.VMEM((arrays, quarter, width), jnp.float32),
            pltpu.VMEM((arrays, quarter, width), kind),
            pltpu.VMEM((arrays, quarter, width), kind),
            pltpu.VMEM((arrays, quarter, channels), kind),
            dma((arrays, 2, 2)),
            dma((arrays, 4, 2)),
            dma((arrays, 4, 2)),
            dma((arrays, 2)),
            dma((arrays, 2)),
        ],
        compiler_params=pltpu.CompilerParams(
            collective_id=collective_id, has_side_effects=True, vmem_limit_bytes=40 * 2**20
        ),
        name="scatter_plane",
    )(*partials)


def butterfly(values):
    count = lax.axis_size("tensor")
    step = 1
    while step < count:
        values = values + lax.ppermute(values, "tensor", [(i, i ^ step) for i in range(count)])
        step *= 2
    return values


def paired_plan(
    image,
    dw_kernel,
    dw_bias,
    norm_gain,
    norm_bias,
    w_expand,
    b_expand,
    w_project,
    b_project,
    layer_scale,
    out_grad,
):
    kernel_size = dw_kernel.shape[0]
    rim_depth = kernel_size // 2
    height, breadth, channels = image.shape
    positions = height * breadth
    features = norm_gain.shape[0]
    half_features = features // 2
    row = lax.axis_index("rows")
    channel_start = lax.axis_index("tensor") * channels
    gain_part = lax.dynamic_slice_in_dim(norm_gain, channel_start, channels)
    gain_half = lax.dynamic_slice_in_dim(norm_gain, row * half_features, half_features)
    shift_half = lax.dynamic_slice_in_dim(norm_bias, row * half_features, half_features)
    upstream = out_grad.reshape(positions, channels).astype(jnp.float32)
    scaled_grad = (upstream * layer_scale).astype(jnp.bfloat16)
    grad_panels = gather_plane(scaled_grad, 0)
    rimmed = extended(image, (("rows", 0),), rim_depth)
    wide_image = jnp.pad(rimmed, ((0, 0), (rim_depth, rim_depth), (0, 0))).astype(jnp.float32)
    convolved = depthwise(wide_image, dw_kernel, height, breadth) + dw_bias
    mixed = convolved.astype(jnp.bfloat16).reshape(positions, channels)
    mixed_panels = gather_plane(mixed, 1)
    hidden_partial = contract_last(grad_panels, w_project)
    hidden_grad = hidden_partial + pair_swap(hidden_partial.astype(jnp.bfloat16))
    mixed_wide = mixed_panels.astype(jnp.float32)
    sums = jnp.stack([jnp.sum(mixed_wide, 1), jnp.sum(mixed_wide * mixed_wide, 1)])
    sums = sums + pair_swap(sums)
    average = sums[0] / features
    inv_std = lax.rsqrt(sums[1] / features - average * average + EPSILON)
    centred_half = (mixed_wide - average[:, None]) * inv_std[:, None]
    normed = (centred_half * gain_half + shift_half).astype(jnp.bfloat16)
    pre_partial = jnp.dot(normed, w_expand, preferred_element_type=jnp.float32)
    pre = pre_partial + pair_swap(pre_partial.astype(jnp.bfloat16)) + b_expand
    pre_grad = (hidden_grad * gelu_slope(pre)).astype(jnp.bfloat16)
    normed_partial = contract_last(pre_grad, w_expand)
    hidden = gelu_exact(pre).astype(jnp.bfloat16)
    partial_out = jnp.dot(hidden, w_project, preferred_element_type=jnp.float32)
    normed_block, projected_block = scatter_plane(
        [normed_partial.astype(jnp.bfloat16), partial_out.astype(jnp.bfloat16)], 2
    )
    normed_grad = normed_block.astype(jnp.float32)
    projected = projected_block.astype(jnp.float32) + b_project
    project_grad = contract_first(hidden, grad_panels)
    expand_grad = contract_first(normed, pre_grad)
    residual = image.reshape(positions, channels).astype(jnp.float32)
    result = (
        (residual + layer_scale * projected).astype(jnp.bfloat16).reshape(height, breadth, channels)
    )
    scale_term = jnp.sum(upstream * projected, 0)
    own_average = lax.dynamic_slice_in_dim(average, row * positions, positions)[:, None]
    own_inv_std = lax.dynamic_slice_in_dim(inv_std, row * positions, positions)[:, None]
    centred = (mixed.astype(jnp.float32) - own_average) * own_inv_std
    gain_grad = normed_grad * gain_part
    totals = butterfly(jnp.stack([jnp.sum(gain_grad, 1), jnp.sum(gain_grad * centred, 1)]))
    plain_mean = totals[0][:, None] / features
    centred_mean = totals[1][:, None] / features
    mixed_grad = (own_inv_std * (gain_grad - plain_mean - centred * centred_mean)).astype(
        jnp.bfloat16
    )
    mixed_grad = mixed_grad.reshape(height, breadth, channels)
    grad_rimmed = extended(mixed_grad, (("rows", 0),), rim_depth)
    wide_grad = jnp.pad(grad_rimmed, ((0, 0), (rim_depth, rim_depth), (0, 0))).astype(jnp.float32)
    back = depthwise(wide_grad, dw_kernel[::-1, ::-1], height, breadth)
    image_grad = (upstream.reshape(height, breadth, channels) + back).astype(jnp.bfloat16)
    kernel_local = kernel_terms(wide_image, mixed_grad.astype(jnp.float32), kernel_size)
    kernel_grad = kernel_local + pair_swap(kernel_local)
    scale_grad = scale_term + pair_swap(scale_term)
    return (result, image_grad, expand_grad, project_grad, kernel_grad, scale_grad)


def solution(mesh):
    paired = mesh.shape["rows"] == 2 and mesh.shape["tensor"] == 16
    return jax.shard_map(
        paired_plan if paired else general_plan,
        mesh=mesh,
        in_specs=(
            P("rows", None, "tensor"),
            P(None, None, "tensor"),
            P("tensor"),
            P(),
            P(),
            P("rows", "tensor"),
            P("tensor"),
            P("tensor", "rows"),
            P("tensor"),
            P("tensor"),
            P("rows", None, "tensor"),
        ),
        out_specs=(
            P("rows", None, "tensor"),
            P("rows", None, "tensor"),
            P("rows", "tensor"),
            P("tensor", "rows"),
            P(None, None, "tensor"),
            P("tensor"),
        ),
        check_vma=False,
    )
```

```python
import functools
import math

import jax
import jax.numpy as jnp
from jax import lax
from jax.experimental import pallas as pl
from jax.experimental.pallas import tpu as pltpu
from jax.sharding import PartitionSpec as P

EPSILON = 1e-06


def extended(cells, sides, width):
    for axis, dim in sides:
        count = lax.axis_size(axis)
        ends = count - 1
        head = lax.slice_in_dim(cells, 0, width, axis=dim)
        tail = lax.slice_in_dim(cells, cells.shape[dim] - width, cells.shape[dim], axis=dim)
        cells = jnp.concatenate(
            [
                lax.ppermute(tail, axis, [(i, (i + 1) % count) for i in range(ends)]),
                cells,
                lax.ppermute(head, axis, [((i + 1) % count, i) for i in range(ends)]),
            ],
            axis=dim,
        )
    return cells


def gelu_exact(values):
    return 0.5 * values * (1.0 + lax.erf(values * (1.0 / math.sqrt(2.0))))


def gelu_slope(values):
    cumulative = 0.5 * (1.0 + lax.erf(values * (1.0 / math.sqrt(2.0))))
    density = jnp.exp(-0.5 * values * values) * (1.0 / math.sqrt(2.0 * math.pi))
    return cumulative + values * density


def depthwise(padded, kernel, height, breadth):
    kernel_size = kernel.shape[0]
    summed = jnp.zeros((height, breadth, kernel.shape[2]), jnp.float32)
    for row_shift in range(kernel_size):
        for col_shift in range(kernel_size):
            window = padded[row_shift : row_shift + height, col_shift : col_shift + breadth]
            summed = summed + kernel[row_shift, col_shift].astype(jnp.float32) * window
    return summed


def kernel_terms(padded, gradient, kernel_size):
    height, breadth = (gradient.shape[0], gradient.shape[1])
    kernel_rows = []
    for row_shift in range(kernel_size):
        kernel_line = []
        for col_shift in range(kernel_size):
            window = padded[row_shift : row_shift + height, col_shift : col_shift + breadth]
            kernel_line.append(jnp.sum(window * gradient, axis=(0, 1)))
        kernel_rows.append(jnp.stack(kernel_line))
    return jnp.stack(kernel_rows)


def contract_last(left, right):
    return lax.dot_general(
        left, right, (((1,), (1,)), ((), ())), preferred_element_type=jnp.float32
    )


def contract_first(left, right):
    return lax.dot_general(
        left, right, (((0,), (0,)), ((), ())), preferred_element_type=jnp.float32
    )


def general_plan(
    image,
    dw_kernel,
    dw_bias,
    norm_gain,
    norm_bias,
    w_expand,
    b_expand,
    w_project,
    b_project,
    layer_scale,
    out_grad,
):
    kernel_size = dw_kernel.shape[0]
    rim_depth = kernel_size // 2
    height, breadth, channels = image.shape
    positions = height * breadth
    features = norm_gain.shape[0]
    channel_start = lax.axis_index("tensor") * channels
    gain_part = lax.dynamic_slice_in_dim(norm_gain, channel_start, channels)
    shift_part = lax.dynamic_slice_in_dim(norm_bias, channel_start, channels)
    rimmed = extended(image, (("rows", 0),), rim_depth)
    wide_image = jnp.pad(rimmed, ((0, 0), (rim_depth, rim_depth), (0, 0))).astype(jnp.float32)
    convolved = depthwise(wide_image, dw_kernel, height, breadth) + dw_bias
    mixed = convolved.astype(jnp.bfloat16).reshape(positions, channels)
    own_mixed = mixed.astype(jnp.float32)
    plain_sum, square_sum = lax.psum(
        (jnp.sum(own_mixed, 1), jnp.sum(own_mixed * own_mixed, 1)), "tensor"
    )
    average = plain_sum[:, None] / features
    inv_std = lax.rsqrt(square_sum[:, None] / features - average * average + EPSILON)
    centred = (own_mixed - average) * inv_std
    normed_part = (centred * gain_part + shift_part).astype(jnp.bfloat16)
    normed = lax.all_gather(normed_part, "tensor", axis=1, tiled=True)
    columns = normed
    pre = jnp.dot(
        columns,
        lax.all_gather(w_expand, "rows", axis=0, tiled=True),
        preferred_element_type=jnp.float32,
    )
    pre = pre + b_expand
    hidden = gelu_exact(pre).astype(jnp.bfloat16)
    partial_out = jnp.dot(
        hidden,
        lax.all_gather(w_project, "rows", axis=1, tiled=True),
        preferred_element_type=jnp.float32,
    )
    projected = (
        lax.psum_scatter(
            partial_out.astype(jnp.bfloat16), "tensor", scatter_dimension=1, tiled=True
        ).astype(jnp.float32)
        + b_project
    )
    residual = image.reshape(positions, channels).astype(jnp.float32)
    result = (
        (residual + layer_scale * projected).astype(jnp.bfloat16).reshape(height, breadth, channels)
    )
    upstream = out_grad.reshape(positions, channels).astype(jnp.float32)
    scale_term = jnp.sum(upstream * projected, 0)
    scaled_grad = (upstream * layer_scale).astype(jnp.bfloat16)
    grad_panels = lax.all_gather(scaled_grad, "tensor", axis=1, tiled=True)
    project_term = contract_first(hidden, grad_panels)
    project_grad = lax.psum_scatter(
        project_term.astype(jnp.bfloat16), "rows", scatter_dimension=1, tiled=True
    ).astype(jnp.float32)
    columns = grad_panels
    hidden_grad = contract_last(columns, lax.all_gather(w_project, "rows", axis=1, tiled=True))
    pre_grad = (hidden_grad * gelu_slope(pre)).astype(jnp.bfloat16)
    columns = normed
    expand_grad = lax.psum_scatter(
        contract_first(columns, pre_grad).astype(jnp.bfloat16),
        "rows",
        scatter_dimension=0,
        tiled=True,
    ).astype(jnp.float32)
    normed_partial = contract_last(pre_grad, lax.all_gather(w_expand, "rows", axis=0, tiled=True))
    normed_grad = lax.psum_scatter(
        normed_partial.astype(jnp.bfloat16), "tensor", scatter_dimension=1, tiled=True
    ).astype(jnp.float32)
    gain_grad = normed_grad * gain_part
    plain_total, centred_total = lax.psum(
        (jnp.sum(gain_grad, 1), jnp.sum(gain_grad * centred, 1)), "tensor"
    )
    plain_mean = plain_total[:, None] / features
    centred_mean = centred_total[:, None] / features
    mixed_grad = (inv_std * (gain_grad - plain_mean - centred * centred_mean)).astype(jnp.bfloat16)
    mixed_grad = mixed_grad.reshape(height, breadth, channels)
    grad_rimmed = extended(mixed_grad, (("rows", 0),), rim_depth)
    wide_grad = jnp.pad(grad_rimmed, ((0, 0), (rim_depth, rim_depth), (0, 0))).astype(jnp.float32)
    back = depthwise(wide_grad, dw_kernel[::-1, ::-1], height, breadth)
    image_grad = (upstream.reshape(height, breadth, channels) + back).astype(jnp.bfloat16)
    kernel_local = kernel_terms(wide_image, mixed_grad.astype(jnp.float32), kernel_size)
    kernel_grad, scale_grad = lax.psum((kernel_local, scale_term), "rows")
    return (result, image_grad, expand_grad, project_grad, kernel_grad, scale_grad)


def pair_swap(value):
    return lax.ppermute(value, "rows", [(0, 1), (1, 0)])


MESH = pl.DeviceIdType.MESH
CHIP_STEPS = (2, 1, 3)


class Place:
    def __init__(self):
        self.tensor = lax.axis_index("tensor")
        self.row = lax.axis_index("rows")
        self.core = lax.rem(self.tensor, 2)
        self.column = lax.rem(self.tensor // 2, 2)
        self.count = lax.axis_size("tensor")
        self.across = self.tensor + 2 - 4 * self.column
        self.sibling = self.tensor + 1 - 2 * self.core
        self.traded = (self.tensor // (self.count // 2)) != self.row
        self.trader = lax.rem(self.tensor + self.count // 2, self.count)

    def along(self, step):
        return lax.rem(self.tensor + 4 * step, self.count)

    def here(self, tensor):
        return (tensor, self.row)

    def meet(self):
        barrier = pltpu.get_barrier_semaphore()
        peers = [self.sibling, self.across] + [self.along(step) for step in CHIP_STEPS]
        for peer in peers:
            pl.semaphore_signal(barrier, inc=1, device_id=self.here(peer), device_id_type=MESH)

        for peer in (self.trader, self.tensor):
            pl.semaphore_signal(
                barrier, inc=1, device_id=(peer, 1 - self.row), device_id_type=MESH
            )
        pl.semaphore_wait(barrier, len(peers) + 2)


def remote(source, target, sems, device):
    return pltpu.make_async_remote_copy(
        src_ref=source,
        dst_ref=target,
        send_sem=sems.at[0],
        recv_sem=sems.at[1],
        device_id=device,
        device_id_type=MESH,
    )


def region(ref, tensor, core, quarter, width, count):
    half = tensor // (count // 2)
    panel = lax.rem(tensor, count // 2) // 2
    rows = pl.ds(pl.multiple_of(half * 2 * quarter + core * quarter, quarter), quarter)
    return ref.at[rows, pl.ds(pl.multiple_of(panel * width, 128), width)]


def gather_kernel(paired, *refs):
    block_ref, out_ref = refs[0], refs[1 + paired]
    arrived, block, pre_sem, swap_sem, z_sem, x_sem, c_sem, pair_sem = refs[2 + 2 * paired :]
    place = Place()
    quarter = block_ref.shape[0] // 2
    width = block.shape[1]

    def spot(tensor):
        return region(out_ref, tensor, place.core, quarter, width, place.count)

    place.meet()
    other_rows = pl.ds(pl.multiple_of((1 - place.core) * quarter, quarter), quarter)
    own_rows = pl.ds(pl.multiple_of(place.core * quarter, quarter), quarter)
    pair_copies = []
    if paired:
        pair_copies.append(
            remote(refs[1], refs[3], pair_sem, (place.tensor, 1 - place.row))
        )
        pair_copies[0].start()
    pairing = remote(block_ref.at[other_rows, :], arrived, pre_sem, place.here(place.sibling))
    pairing.start()
    pairing.wait()

    @pl.when(place.core == 0)
    def _():
        block[...] = jnp.concatenate([block_ref[own_rows, :], arrived[...]], axis=1)

    @pl.when(place.core == 1)
    def _():
        block[...] = jnp.concatenate([arrived[...], block_ref[own_rows, :]], axis=1)

    @pl.when(place.traded)
    def _():
        swap = remote(block, spot(place.trader), swap_sem, (place.trader, 1 - place.row))
        swap.start()
        swap.wait()

    @pl.when(jnp.logical_not(place.traded))
    def _():
        keep = pltpu.make_async_copy(block, spot(place.tensor), swap_sem.at[0])
        keep.start()
        keep.wait()

    mine = spot(place.tensor)
    z_copies = [
        remote(mine, mine, z_sem.at[step], place.here(place.along(step))) for step in CHIP_STEPS
    ]
    for copy in z_copies:
        copy.start()
    x_copies, c_copies = [], []
    for index, step in enumerate((0,) + CHIP_STEPS):
        if step:
            z_copies[index - 1].wait_recv()
        origin = lax.rem(place.tensor + 4 * (4 - step), place.count)
        chunk = spot(origin)
        x_copies.append(remote(chunk, chunk, x_sem.at[index], place.here(place.across)))
        c_copies.append(remote(chunk, chunk, c_sem.at[index], place.here(place.sibling)))
        x_copies[-1].start()
        c_copies[-1].start()
    for index, step in enumerate((0,) + CHIP_STEPS):
        x_copies[index].wait_recv()
        origin = lax.rem(place.across + 4 * (4 - step), place.count)
        chunk = spot(origin)
        c_copies.append(remote(chunk, chunk, c_sem.at[4 + index], place.here(place.sibling)))
        c_copies[-1].start()
    for copy in c_copies + pair_copies:
        copy.wait_recv()
    for copy in pair_copies + z_copies + x_copies + c_copies:
        copy.wait_send()


def gather_plane(block, collective_id, pair=()):
    count = lax.axis_size("tensor")
    positions, channels = block.shape
    quarter, width = positions // 2, 2 * channels
    dma = pltpu.SemaphoreType.DMA
    vmem = pl.BlockSpec(memory_space=pltpu.VMEM)
    gathered = jax.ShapeDtypeStruct((2 * positions, count // 2 * channels), block.dtype)
    return pl.pallas_call(
        functools.partial(gather_kernel, len(pair)),
        out_shape=[gathered] + [jax.ShapeDtypeStruct(p.shape, p.dtype) for p in pair],
        in_specs=[vmem] * (1 + len(pair)),
        out_specs=[vmem] * (1 + len(pair)),
        scratch_shapes=[
            pltpu.VMEM((quarter, channels), block.dtype),
            pltpu.VMEM((quarter, width), block.dtype),
            dma((2,)),
            dma((2,)),
            dma((4, 2)),
            dma((4, 2)),
            dma((8, 2)),
            dma((2,)),
        ],
        compiler_params=pltpu.CompilerParams(
            collective_id=collective_id, has_side_effects=True, vmem_limit_bytes=24 * 2**20
        ),
        name="gather_plane",
    )(block, *pair)


def scatter_kernel(arrays, *refs):
    partials, outs = refs[:arrays], refs[arrays : 2 * arrays]
    from_core, to_x, from_x, to_z, from_z, kept, final, swapped, leaving = refs[
        2 * arrays : 2 * arrays + 9
    ]
    c_sem, x_sem, z_sem, swap_sem, end_sem = refs[2 * arrays + 9 :]
    place = Place()
    quarter, width = final.shape[1:]
    channels = width // 2
    place.meet()
    copies = []
    c_copies = []
    for a in range(arrays):
        for half in range(2):
            start = half * 2 * quarter + (1 - place.core) * quarter
            rows = pl.ds(pl.multiple_of(start, quarter), quarter)
            copy = remote(
                partials[a].at[rows, :],
                from_core.at[a, half],
                c_sem.at[a, half],
                place.here(place.sibling),
            )
            copy.start()
            c_copies.append(copy)

    def chip_sum(a, tensor):
        half = tensor // (place.count // 2)
        panel = lax.rem(tensor, place.count // 2) // 2
        lanes = pl.ds(pl.multiple_of(panel * width, 128), width)
        start = half * 2 * quarter + place.core * quarter
        rows = pl.ds(pl.multiple_of(start, quarter), quarter)
        own = partials[a][rows, lanes].astype(jnp.float32)
        return own + from_core[a, half, :, lanes].astype(jnp.float32)

    x_copies, z_copies = {}, {}
    for a in range(arrays):
        c_copies[2 * a].wait_recv()
        c_copies[2 * a + 1].wait_recv()
        for step in CHIP_STEPS + (0,):
            target = lax.rem(place.across + 4 * step, place.count)
            to_x[a, step] = chip_sum(a, target).astype(to_x.dtype)
            copy = remote(
                to_x.at[a, step], from_x.at[a, step], x_sem.at[a, step], place.here(place.across)
            )
            copy.start()
            x_copies[a, step] = copy
    for a in range(arrays):
        for step in CHIP_STEPS + (0,):
            target = place.along(step)
            x_copies[a, step].wait_recv()
            summed = chip_sum(a, target) + from_x[a, step].astype(jnp.float32)
            if step:
                to_z[a, step] = summed.astype(to_z.dtype)
                copy = remote(
                    to_z.at[a, step], from_z.at[a, step], z_sem.at[a, step], place.here(target)
                )
                copy.start()
                z_copies[a, step] = copy
            else:
                kept[a] = summed
    swaps = []
    for a in range(arrays):
        summed = kept[a]
        for step in CHIP_STEPS:
            z_copies[a, step].wait_recv()
            summed = summed + from_z[a, step].astype(jnp.float32)
        final[a] = summed.astype(final.dtype)
        swap = remote(
            final.at[a], swapped.at[a], swap_sem.at[a], (place.trader, 1 - place.row)
        )
        swaps.append(swap)

        @pl.when(place.traded)
        def _():
            swap.start()

    ends = []
    own_rows = pl.ds(pl.multiple_of(place.core * quarter, quarter), quarter)
    for a in range(arrays):

        @pl.when(place.traded)
        def _():
            swaps[a].wait()

        @pl.when(jnp.logical_not(place.traded))
        def _():
            swapped[a] = final[a]

        @pl.when(place.core == 0)
        def _():
            outs[a][own_rows, :] = swapped[a][:, :channels]
            leaving[a] = swapped[a][:, channels:]

        @pl.when(place.core == 1)
        def _():
            outs[a][own_rows, :] = swapped[a][:, channels:]
            leaving[a] = swapped[a][:, :channels]

        copy = remote(
            leaving.at[a], outs[a].at[own_rows, :], end_sem.at[a], place.here(place.sibling)
        )
        copy.start()
        ends.append(copy)
    for copy in ends:
        copy.wait()
    for copy in c_copies + list(x_copies.values()) + list(z_copies.values()):
        copy.wait_send()


def scatter_plane(partials, collective_id):
    count = lax.axis_size("tensor")
    arrays = len(partials)
    positions, channels = partials[0].shape[0] // 2, partials[0].shape[1] // (count // 2)
    quarter, width = positions // 2, 2 * channels
    dma = pltpu.SemaphoreType.DMA
    kind = partials[0].dtype
    vmem = pl.BlockSpec(memory_space=pltpu.VMEM)
    return pl.pallas_call(
        functools.partial(scatter_kernel, arrays),
        out_shape=[jax.ShapeDtypeStruct((positions, channels), kind)] * arrays,
        in_specs=[vmem] * arrays,
        out_specs=[vmem] * arrays,
        scratch_shapes=[
            pltpu.VMEM((arrays, 2, quarter, partials[0].shape[1]), kind),
            pltpu.VMEM((arrays, 4, quarter, width), kind),
            pltpu.VMEM((arrays, 4, quarter, width), kind),
            pltpu.VMEM((arrays, 4, quarter, width), kind),
            pltpu.VMEM((arrays, 4, quarter, width), kind),
            pltpu.VMEM((arrays, quarter, width), jnp.float32),
            pltpu.VMEM((arrays, quarter, width), kind),
            pltpu.VMEM((arrays, quarter, width), kind),
            pltpu.VMEM((arrays, quarter, channels), kind),
            dma((arrays, 2, 2)),
            dma((arrays, 4, 2)),
            dma((arrays, 4, 2)),
            dma((arrays, 2)),
            dma((arrays, 2)),
        ],
        compiler_params=pltpu.CompilerParams(
            collective_id=collective_id, has_side_effects=True, vmem_limit_bytes=40 * 2**20
        ),
        name="scatter_plane",
    )(*partials)


def total_kernel(in_ref, out_ref, held, from_core, from_x, from_z, c_sem, x_sem, z_sem):
    place = Place()
    place.meet()
    c_copy = remote(in_ref, from_core, c_sem, place.here(place.sibling))
    c_copy.start()
    c_copy.wait()
    held[0] = in_ref[...] + from_core[...]
    x_copy = remote(held.at[0], from_x, x_sem, place.here(place.across))
    x_copy.start()
    x_copy.wait()
    held[1] = held[0] + from_x[...]
    z_copies = []
    for step in CHIP_STEPS:
        copy = remote(
            held.at[1], from_z.at[step], z_sem.at[step], place.here(place.along(step))
        )
        copy.start()
        z_copies.append(copy)
    for copy in z_copies:
        copy.wait()
    out_ref[...] = held[1] + from_z[1] + from_z[2] + from_z[3]


def total_over_tensor(values, collective_id):
    dma = pltpu.SemaphoreType.DMA
    vmem = pl.BlockSpec(memory_space=pltpu.VMEM)
    return pl.pallas_call(
        total_kernel,
        out_shape=jax.ShapeDtypeStruct(values.shape, values.dtype),
        in_specs=[vmem],
        out_specs=vmem,
        scratch_shapes=[
            pltpu.VMEM((2, *values.shape), values.dtype),
            pltpu.VMEM(values.shape, values.dtype),
            pltpu.VMEM(values.shape, values.dtype),
            pltpu.VMEM((4, *values.shape), values.dtype),
            dma((2,)),
            dma((2,)),
            dma((4, 2)),
        ],
        compiler_params=pltpu.CompilerParams(collective_id=collective_id, has_side_effects=True),
        name="total_over_tensor",
    )(values)


def paired_plan(
    image,
    dw_kernel,
    dw_bias,
    norm_gain,
    norm_bias,
    w_expand,
    b_expand,
    w_project,
    b_project,
    layer_scale,
    out_grad,
):
    kernel_size = dw_kernel.shape[0]
    rim_depth = kernel_size // 2
    height, breadth, channels = image.shape
    positions = height * breadth
    features = norm_gain.shape[0]
    half_features = features // 2
    row = lax.axis_index("rows")
    channel_start = lax.axis_index("tensor") * channels
    gain_part = lax.dynamic_slice_in_dim(norm_gain, channel_start, channels)
    gain_half = lax.dynamic_slice_in_dim(norm_gain, row * half_features, half_features)
    shift_half = lax.dynamic_slice_in_dim(norm_bias, row * half_features, half_features)
    upstream = out_grad.reshape(positions, channels).astype(jnp.float32)
    scaled_grad = (upstream * layer_scale).astype(jnp.bfloat16)
    (grad_panels,) = gather_plane(scaled_grad, 0)
    rimmed = extended(image, (("rows", 0),), rim_depth)
    wide_image = jnp.pad(rimmed, ((0, 0), (rim_depth, rim_depth), (0, 0))).astype(jnp.float32)
    convolved = depthwise(wide_image, dw_kernel, height, breadth) + dw_bias
    mixed = convolved.astype(jnp.bfloat16).reshape(positions, channels)
    hidden_partial = contract_last(grad_panels, w_project)
    mixed_panels, hidden_other = gather_plane(mixed, 1, (hidden_partial.astype(jnp.bfloat16),))
    hidden_grad = hidden_partial + hidden_other
    mixed_wide = mixed_panels.astype(jnp.float32)
    sums = jnp.stack([jnp.sum(mixed_wide, 1), jnp.sum(mixed_wide * mixed_wide, 1)])
    sums = sums + pair_swap(sums)
    average = sums[0] / features
    inv_std = lax.rsqrt(sums[1] / features - average * average + EPSILON)
    centred_half = (mixed_wide - average[:, None]) * inv_std[:, None]
    normed = (centred_half * gain_half + shift_half).astype(jnp.bfloat16)
    pre_partial = jnp.dot(normed, w_expand, preferred_element_type=jnp.float32)
    pre = pre_partial + pair_swap(pre_partial.astype(jnp.bfloat16)) + b_expand
    pre_grad = (hidden_grad * gelu_slope(pre)).astype(jnp.bfloat16)
    normed_partial = contract_last(pre_grad, w_expand)
    hidden = gelu_exact(pre).astype(jnp.bfloat16)
    partial_out = jnp.dot(hidden, w_project, preferred_element_type=jnp.float32)
    normed_block, projected_block = scatter_plane(
        [normed_partial.astype(jnp.bfloat16), partial_out.astype(jnp.bfloat16)], 2
    )
    normed_grad = normed_block.astype(jnp.float32)
    projected = projected_block.astype(jnp.float32) + b_project
    project_grad = contract_first(hidden, grad_panels)
    expand_grad = contract_first(normed, pre_grad)
    residual = image.reshape(positions, channels).astype(jnp.float32)
    result = (
        (residual + layer_scale * projected).astype(jnp.bfloat16).reshape(height, breadth, channels)
    )
    scale_term = jnp.sum(upstream * projected, 0)
    own_average = lax.dynamic_slice_in_dim(average, row * positions, positions)[:, None]
    own_inv_std = lax.dynamic_slice_in_dim(inv_std, row * positions, positions)[:, None]
    centred = (mixed.astype(jnp.float32) - own_average) * own_inv_std
    gain_grad = normed_grad * gain_part
    totals = total_over_tensor(
        jnp.stack([jnp.sum(gain_grad, 1), jnp.sum(gain_grad * centred, 1)]), 3
    )
    plain_mean = totals[0][:, None] / features
    centred_mean = totals[1][:, None] / features
    mixed_grad = (own_inv_std * (gain_grad - plain_mean - centred * centred_mean)).astype(
        jnp.bfloat16
    )
    mixed_grad = mixed_grad.reshape(height, breadth, channels)
    grad_rimmed = extended(mixed_grad, (("rows", 0),), rim_depth)
    wide_grad = jnp.pad(grad_rimmed, ((0, 0), (rim_depth, rim_depth), (0, 0))).astype(jnp.float32)
    back = depthwise(wide_grad, dw_kernel[::-1, ::-1], height, breadth)
    image_grad = (upstream.reshape(height, breadth, channels) + back).astype(jnp.bfloat16)
    kernel_local = kernel_terms(wide_image, mixed_grad.astype(jnp.float32), kernel_size)
    kernel_grad = kernel_local + pair_swap(kernel_local)
    scale_grad = scale_term + pair_swap(scale_term)
    return (result, image_grad, expand_grad, project_grad, kernel_grad, scale_grad)


def solution(mesh):
    paired = mesh.shape["rows"] == 2 and mesh.shape["tensor"] == 16
    return jax.shard_map(
        paired_plan if paired else general_plan,
        mesh=mesh,
        in_specs=(
            P("rows", None, "tensor"),
            P(None, None, "tensor"),
            P("tensor"),
            P(),
            P(),
            P("rows", "tensor"),
            P("tensor"),
            P("tensor", "rows"),
            P("tensor"),
            P("tensor"),
            P("rows", None, "tensor"),
        ),
        out_specs=(
            P("rows", None, "tensor"),
            P("rows", None, "tensor"),
            P("rows", "tensor"),
            P("tensor", "rows"),
            P(None, None, "tensor"),
            P("tensor"),
        ),
        check_vma=False,
    )
```
